256 devices in a mesh: fsdp: 16 (over z, x_lo), tensor: 16 (over x_hi, y, core).
Axes of the slice: x: 4 (x_hi: 2, x_lo: 2; x = x_hi * 2 + x_lo), y: 4, z: 8, core: 2. Of those that a mesh axis runs over, the one named last changes fastest.
Arguments:
- tokens: bfloat16 [768, 6144], P('tensor', 'fsdp'), may hold values from -128 to 128
- cotangent: bfloat16 [768, 6144], P('tensor', 'fsdp'), may hold values from -0.29882812 to 0.29882812
- up_weight: bfloat16 [6144, 24576], P('fsdp', 'tensor'), may hold values from -0.078125 to 0.078125
- up_probe: bfloat16 [6144, 24576], P('fsdp', 'tensor'), may hold values from -5 to 5
- down_weight: bfloat16 [24576, 6144], P('tensor', 'fsdp'), may hold values from -0.0390625 to 0.0390625
- down_probe: bfloat16 [24576, 6144], P('tensor', 'fsdp'), may hold values from -5 to 5
Outputs:
- grad_up: bfloat16 [6144, 24576], P('fsdp', 'tensor')
- hess_up: bfloat16 [6144, 24576], P('fsdp', 'tensor')
- grad_down: bfloat16 [24576, 6144], P('tensor', 'fsdp')
- hess_down: bfloat16 [24576, 6144], P('tensor', 'fsdp')
The draws below stay inside these ranges and needn't reach their ends.
All inputs are finite; a program needn't handle non-finite values.
Results may differ from the reference program's by a relative error of at most 0.035.
Values may be sent and summed in bfloat16 or wider, within the bound.
No kernel may reach another device: no remote copies, remote signals or barrier semaphores. Data moves between devices by JAX's collectives and lax.ppermute only.
A program may use at most 128 MiB of HBM per device.

```python
import jax
import jax.numpy as jnp
from jax import lax

D = 6144
FF = 24576
TOKENS = 768
N_FSDP = 16


def draw_tokens(key, part):
    key = jax.random.fold_in(key, 11)
    keys = jax.random.split(key, 3)
    position = jnp.arange(D, dtype=jnp.float32) / D
    rising = jnp.exp(jnp.log(3.0) * position)[None, :]
    feature_scale = jnp.exp(jax.random.uniform(keys[1], (1, D), minval=-1.15, maxval=1.15))
    row_scale = jnp.exp(jax.random.uniform(keys[2], (TOKENS, 1), minval=-1.15, maxval=1.15))
    base = jax.random.truncated_normal(keys[0], -4.0, 4.0, (TOKENS, D))
    values = base * feature_scale * rising * row_scale
    return values.astype(jnp.float32).astype(jnp.bfloat16)


def shard_levels(own_key, extent, cuts, least, high):
    loudness, own = 1.0, jax.random.fold_in(own_key, 6)
    for dim, shards_of in cuts:
        steps = jnp.exp(jax.random.uniform(jax.random.fold_in(own, dim), (shards_of,), jnp.float32, least / len(cuts), high / len(cuts)))
        loudness = loudness * jnp.repeat(steps, extent[dim] // shards_of).reshape([-1 if axis == dim else 1 for axis in range(len(extent))])
    return loudness


def gaussian(rng, shape, scale, reach, cuts=(), kind=jnp.bfloat16):
    entries = jax.random.normal(rng, shape, jnp.float32) * scale
    if len(cuts) > 0:
        entries = shard_levels(rng, shape, cuts, -0.22, 0.18) * entries
    return jnp.clip(entries, min=-reach, max=reach).astype(kind)


def setup_inputs(seed: int = 0) -> dict:
    key_of = jax.random.split(jax.random.key(seed), 7)
    tokens = draw_tokens(jax.random.fold_in(key_of[6], 71), 0)
    cotangent = gaussian(key_of[1], (TOKENS, D), 0.05, 0.29882812, ((0, 16), (1, 16)))
    up_weight = gaussian(key_of[2], (D, FF), D ** -0.5, 0.078125, ((0, 16), (1, 16)))
    up_probe = gaussian(key_of[3], (D, FF), 1.0, 5.0, ((0, 16), (1, 16)))
    down_weight = gaussian(key_of[4], (FF, D), FF ** -0.5, 0.0390625, ((0, 16), (1, 16)))
    down_probe = gaussian(key_of[5], (FF, D), 1.0, 5.0, ((0, 16), (1, 16)))
    return {"tokens": tokens, "cotangent": cotangent, "up_weight": up_weight, "up_probe": up_probe, "down_weight": down_weight, "down_probe": down_probe}


epsilon = 1e-05
inv_root_two = 0.7071067811865476
inv_root_tau = 0.3989422804014327

def normalize(tokens):
    values = tokens.astype(jnp.float32)
    row_mean = lax.optimization_barrier(jnp.mean(values, axis=1, keepdims=True))
    row_square = lax.optimization_barrier(jnp.mean(values * values, axis=1, keepdims=True))
    row_var = row_square - row_mean * row_mean
    return ((values - row_mean) * lax.rsqrt(row_var + epsilon)).astype(jnp.bfloat16)

def activations(sums, width):
    pre_act = sums[:, :width]
    tangent = sums[:, width:2 * width]
    back_grad = sums[:, 2 * width:3 * width]
    tangent_back = sums[:, 3 * width:]
    cumulative = 0.5 * (1.0 + lax.erf(pre_act * inv_root_two))
    density = jnp.exp(-0.5 * pre_act * pre_act) * inv_root_tau
    slope = cumulative + pre_act * density
    curve = density * (2.0 - pre_act * pre_act)
    hidden = (pre_act * cumulative).astype(jnp.bfloat16)
    tangent_hidden = (slope * tangent).astype(jnp.bfloat16)
    grad_pre = (back_grad * slope).astype(jnp.bfloat16)
    tangent_pre = (tangent_back * slope + back_grad * curve * tangent).astype(jnp.bfloat16)
    return (grad_pre, tangent_pre, hidden, tangent_hidden)

def reference(tokens, cotangent, up_weight, up_probe, down_weight, down_probe):
    normed = normalize(tokens)
    block_width = D // N_FSDP
    normed_blocks = normed.reshape(TOKENS, N_FSDP, block_width).transpose(1, 0, 2)
    cot_blocks = cotangent.reshape(TOKENS, N_FSDP, block_width).transpose(1, 0, 2)
    up_pair = jnp.concatenate([up_weight, up_probe], axis=1).reshape(N_FSDP, block_width, 2 * FF)
    down_pair = jnp.concatenate([down_weight, down_probe], axis=0).reshape(2 * FF, N_FSDP, block_width).transpose(1, 0, 2)

    def accumulate(totals, blocks):
        normed_part, cot_part, up_part, down_part = blocks
        forward = jnp.dot(normed_part, up_part, preferred_element_type=jnp.float32)
        backward = lax.dot_general(cot_part, down_part, (((1,), (1,)), ((), ())), preferred_element_type=jnp.float32)
        rounded = lax.optimization_barrier(jnp.concatenate([forward, backward], axis=1).astype(jnp.bfloat16))
        return (totals + rounded.astype(jnp.float32), None)
    sums, _ = lax.scan(accumulate, jnp.zeros((TOKENS, 4 * FF), jnp.float32), (normed_blocks, cot_blocks, up_pair, down_pair))
    grad_pre, tangent_pre, hidden, tangent_hidden = activations(sums, FF)
    up_sums = jnp.dot(normed.T, jnp.concatenate([grad_pre, tangent_pre], axis=1), preferred_element_type=jnp.float32)
    down_sums = jnp.dot(jnp.concatenate([hidden, tangent_hidden], axis=1).T, cotangent, preferred_element_type=jnp.float32)
    grad_up = up_sums[:, :FF].astype(jnp.bfloat16)
    hess_up = (up_probe.astype(jnp.float32) * up_sums[:, FF:]).astype(jnp.bfloat16)
    grad_down = down_sums[:FF].astype(jnp.bfloat16)
    hess_down = (down_probe.astype(jnp.float32) * down_sums[FF:]).astype(jnp.bfloat16)
    return (grad_up, hess_up, grad_down, hess_down)
```

```python
import jax
import jax.numpy as jnp
from jax import lax
from jax.sharding import PartitionSpec as P

epsilon = 1e-05
inv_root_two = 0.7071067811865476
inv_root_tau = 0.3989422804014327

BOTH = ("fsdp", "tensor")
F32 = jnp.float32
BF16 = jnp.bfloat16


def pairs_of(move):
    pairs = []
    for fsdp in range(16):
        for tensor in range(16):
            x, y, z, core = (tensor // 8) * 2 + fsdp % 2, (tensor // 2) % 4, fsdp // 2, tensor % 2
            x, y, z, core = move(x, y, z, core)
            target = (z % 8 * 2 + x % 2) * 16 + (x // 2) * 8 + y * 2 + core
            pairs.append((fsdp * 16 + tensor, target))
    return pairs


MAIN = pairs_of(lambda x, y, z, c: (x, y, z + 1 - 2 * c, c))
MINOR = pairs_of(lambda x, y, z, c: (x, y, z - 1 + 2 * c, c))
PARTNER = pairs_of(lambda x, y, z, c: (x ^ 1, y, z, c))
CORES = pairs_of(lambda x, y, z, c: (x, y, z, c ^ 1))
FIRST = [pairs_of(lambda x, y, z, c, k=k: (x ^ (k * c), y ^ (k * (1 - c)), z, c)) for k in (1, 2, 3)]
SECOND = [pairs_of(lambda x, y, z, c, k=k: (x ^ (k * (1 - c)), y ^ (k * c), z, c)) for k in (1, 2, 3)]
DOUBLING = [pairs_of(lambda x, y, z, c, k=k: (x, y, z ^ k, c)) for k in (1, 2, 4)]


def send(value, pairs):
    return lax.ppermute(value, BOTH, pairs)


def add(one, two):
    return (one.astype(F32) + two.astype(F32)).astype(BF16)


def gather_plane(tokens, cotangent, core):
    first = core == 0
    kept, given = jnp.where(first, cotangent, tokens), jnp.where(first, tokens, cotangent)
    taken = send(given, CORES)
    rows = jnp.concatenate([jnp.where(first, kept, taken), jnp.where(first, taken, kept)], axis=0)
    line = jnp.stack([rows] + [send(rows, pairs) for pairs in FIRST])
    plane = jnp.stack([line] + [send(line, pairs) for pairs in SECOND])
    other = send(plane, CORES)
    cot = jnp.where(first, plane, other)
    tok = jnp.where(first, other, plane).swapaxes(0, 1)
    return tok, cot


def split_features(plane):
    width = plane.shape[-1]
    own = jnp.concatenate([plane[0], plane[2]], axis=0).reshape(-1, width)
    far = jnp.concatenate([plane[1], plane[3]], axis=0).reshape(-1, width)
    return own, far


def block(rows, z, step, sign):
    count = rows.shape[0] // 8
    return lax.dynamic_slice_in_dim(rows, lax.rem(z + sign * step + 16, 8) * count, count, 0)


def reduce_z(parts, z, sign):
    main = [block(p, z, 4, sign) for p in parts]
    minor = [block(p, z, -3, sign) for p in parts]
    for step in range(4):
        main = [send(m, MAIN) for m in main]
        if step < 3:
            minor = [send(m, MINOR) for m in minor]
            main = [add(m, block(p, z, 3 - step, sign)) for m, p in zip(main, parts)]
        if step < 2:
            minor = [add(m, block(p, z, step - 2, sign)) for m, p in zip(minor, parts)]
    return [
        a.astype(F32) + b.astype(F32) + block(p, z, 0, sign).astype(F32)
        for a, b, p in zip(main, minor, parts)
    ]


ORDER = (0, -1, 1, -2, 2, -3, 3, -4)


def gather_z(parts):
    outs, main, minor = [[p] for p in parts], list(parts), list(parts)
    for step in range(4):
        main = [send(m, MAIN) for m in main]
        for out, m in zip(outs, main):
            out.append(m)
        if step < 3:
            minor = [send(m, MINOR) for m in minor]
            for out, m in zip(outs, minor):
                out.append(m)
    return [jnp.concatenate(out, axis=0) for out in outs]


def normalize(tok_own, tok_far, full_width):
    own, far = tok_own.astype(F32), tok_far.astype(F32)
    sums = jnp.stack(
        [jnp.sum(own, axis=1) + jnp.sum(far, axis=1), jnp.sum(own * own, axis=1) + jnp.sum(far * far, axis=1)]
    )
    for pairs in DOUBLING:
        sums = sums + send(sums, pairs)
    mean = (sums[0] / full_width)[:, None]
    scale = lax.rsqrt((sums[1] / full_width)[:, None] - mean * mean + epsilon)
    return ((own - mean) * scale).astype(BF16), ((far - mean) * scale).astype(BF16)


def activations(forward, backward):
    width = forward.shape[1] // 2
    pre_act, tangent = forward[:, :width], forward[:, width:]
    back_grad, tangent_back = backward[:, :width], backward[:, width:]
    cumulative = 0.5 * (1.0 + lax.erf(pre_act * inv_root_two))
    density = jnp.exp(-0.5 * pre_act * pre_act) * inv_root_tau
    slope = cumulative + pre_act * density
    curve = density * (2.0 - pre_act * pre_act)
    hidden = (pre_act * cumulative).astype(BF16)
    tangent_hidden = (slope * tangent).astype(BF16)
    grad_pre = (back_grad * slope).astype(BF16)
    tangent_pre = (tangent_back * slope + back_grad * curve * tangent).astype(BF16)
    return jnp.concatenate([grad_pre, tangent_pre], axis=1), jnp.concatenate([hidden, tangent_hidden], axis=1)


def dot(one, two, one_dim, two_dim):
    return lax.dot_general(one, two, (((one_dim,), (two_dim,)), ((), ())), preferred_element_type=F32)


CHUNKS = 2


def on_device(tokens, cotangent, up_weight, up_probe, down_weight, down_probe):
    full_width = tokens.shape[1] * lax.axis_size("fsdp")
    fsdp = lax.axis_index("fsdp")
    z, half = fsdp // 2, fsdp % 2
    core = lax.axis_index("tensor") % 2
    sign = 1 - 2 * core
    hidden = up_weight.shape[1]
    wide = hidden // 2 // CHUNKS

    def columns(chunk, which):
        start = which * (hidden // 2) + chunk * wide
        return jnp.concatenate([lax.dynamic_slice_in_dim(a, start, wide, 1) for a in (up_weight, up_probe)], axis=1)

    def rows(chunk, which):
        start = which * (hidden // 2) + chunk * wide
        return jnp.concatenate([lax.dynamic_slice_in_dim(a, start, wide, 0) for a in (down_weight, down_probe)], axis=0)

    tok, cot = gather_plane(tokens, cotangent, core)
    cot_own, cot_far = split_features(cot)
    tok_own, tok_far = split_features(tok)
    normed_own, normed_far = normalize(tok_own, tok_far, full_width)

    down_own = [rows(i, half) for i in range(CHUNKS)]
    down_far = [send(rows(i, 1 - half), PARTNER) for i in range(CHUNKS)]
    up_own = [columns(i, half) for i in range(CHUNKS)]
    up_far = [send(columns(i, 1 - half), PARTNER) for i in range(CHUNKS)]

    backward = [(dot(cot_own, a, 1, 1) + dot(cot_far, b, 1, 1)).astype(BF16) for a, b in zip(down_own, down_far)]
    backward = reduce_z(backward, z, sign)
    forward = [(dot(normed_own, a, 1, 0) + dot(normed_far, b, 1, 0)).astype(BF16) for a, b in zip(up_own, up_far)]
    forward = reduce_z(forward, z, sign)

    def relative(own, far):
        both = jnp.concatenate([own, far], axis=1)
        return jnp.concatenate([block(both, z, step, sign) for step in ORDER], axis=0)

    normed_rows = relative(normed_own, normed_far)
    cot_rows = relative(cot_own, cot_far)
    width = up_weight.shape[0]
    kept, taken = [], []
    for i in range(CHUNKS):
        up_part, down_part = gather_z(activations(forward[i], backward[i]))
        up_total = dot(normed_rows, up_part, 0, 0)
        down_total = dot(down_part, cot_rows, 0, 0)
        grad_up = up_total[:, :wide].astype(BF16)
        hess_up = (jnp.concatenate([up_own[i], up_far[i]], axis=0)[:, wide:].astype(F32) * up_total[:, wide:]).astype(BF16)
        grad_down = down_total[:wide].astype(BF16)
        hess_down = (jnp.concatenate([down_own[i], down_far[i]], axis=1)[wide:].astype(F32) * down_total[wide:]).astype(BF16)
        kept.append((grad_up[:width], hess_up[:width], grad_down[:, :width], hess_down[:, :width]))
        up_sent = send(jnp.stack([grad_up[width:], hess_up[width:]]), PARTNER)
        down_sent = send(jnp.stack([grad_down[:, width:], hess_down[:, width:]]), PARTNER)
        taken.append((up_sent[0], up_sent[1], down_sent[0], down_sent[1]))

    outs = []
    for which, axis in enumerate((1, 1, 0, 0)):
        mine = [k[which] for k in kept]
        theirs = [t[which] for t in taken]
        outs.append(
            jnp.where(half == 0, jnp.concatenate(mine + theirs, axis=axis), jnp.concatenate(theirs + mine, axis=axis))
        )
    return tuple(outs)


def solution(mesh):
    in_specs = (
        P("tensor", "fsdp"),
        P("tensor", "fsdp"),
        P("fsdp", "tensor"),
        P("fsdp", "tensor"),
        P("tensor", "fsdp"),
        P("tensor", "fsdp"),
    )
    out_specs = (P("fsdp", "tensor"), P("fsdp", "tensor"), P("tensor", "fsdp"), P("tensor", "fsdp"))
    return jax.shard_map(
        on_device, mesh=mesh, in_specs=in_specs, out_specs=out_specs, check_vma=False
    )
```

```python
import jax
import jax.numpy as jnp
from jax import lax
from jax.experimental import pallas as pl
from jax.experimental.pallas import tpu as pltpu
from jax.sharding import PartitionSpec as P

epsilon = 1e-05
inv_root_two = 0.7071067811865476
inv_root_tau = 0.3989422804014327

BOTH = ("fsdp", "tensor")
F32 = jnp.float32
BF16 = jnp.bfloat16


def pairs_of(move):
    pairs = []
    for fsdp in range(16):
        for tensor in range(16):
            x, y, z, core = (tensor // 8) * 2 + fsdp % 2, (tensor // 2) % 4, fsdp // 2, tensor % 2
            x, y, z, core = move(x, y, z, core)
            target = (z % 8 * 2 + x % 2) * 16 + (x // 2) * 8 + y * 2 + core
            pairs.append((fsdp * 16 + tensor, target))
    return pairs


MAIN = pairs_of(lambda x, y, z, c: (x, y, z + 1 - 2 * c, c))
MINOR = pairs_of(lambda x, y, z, c: (x, y, z - 1 + 2 * c, c))
PARTNER = pairs_of(lambda x, y, z, c: (x ^ 1, y, z, c))
CORES = pairs_of(lambda x, y, z, c: (x, y, z, c ^ 1))
FIRST = [pairs_of(lambda x, y, z, c, k=k: (x ^ k, y, z, c)) for k in (1, 2, 3)]
SECOND = [pairs_of(lambda x, y, z, c, k=k: (x, y ^ k, z, c)) for k in (1, 2, 3)]
DOUBLING = [pairs_of(lambda x, y, z, c, k=k: (x, y, z ^ k, c)) for k in (1, 2, 4)]


def send(value, pairs):
    return lax.ppermute(value, BOTH, pairs)


def add(one, two):
    return (one.astype(F32) + two.astype(F32)).astype(BF16)


ORDER = (0, -1, 1, -2, 2, -3, 3, -4)
HBM = pl.BlockSpec(memory_space=pltpu.HBM)
VMEM = pl.BlockSpec(memory_space=pltpu.VMEM)
SMEM = pl.BlockSpec(memory_space=pltpu.SMEM)


def call(kernel, outs, out_specs, scratch, args, specs, aliases=None, flops=0):
    return pl.pallas_call(
        kernel,
        out_shape=outs,
        in_specs=specs,
        out_specs=out_specs,
        scratch_shapes=scratch,
        input_output_aliases=aliases or {},
        compiler_params=pltpu.CompilerParams(vmem_limit_bytes=40 * 2**20),
        cost_estimate=pl.CostEstimate(flops=flops, bytes_accessed=1024, transcendentals=0),
    )(*args)


def shape(*dims, dtype=BF16):
    return jax.ShapeDtypeStruct(dims, dtype)


def run_copies(pairs, sems):
    copies = [pltpu.make_async_copy(src, dst, sems.at[i]) for i, (src, dst) in enumerate(pairs)]
    for copy in copies:
        copy.start()
    return copies


def wait_all(copies):
    for copy in copies:
        copy.wait()


def widths(share):
    return share * 2 // 3, share - share * 2 // 3


def pack(place, weight, probe, axis):
    share = weight.shape[axis] // 2
    wide, _ = widths(share)
    dims = (wide, weight.shape[1]) if axis == 0 else (weight.shape[0], wide)

    def kernel(place_ref, weight_ref, probe_ref, out_ref, sems):
        units = pl.ds(pl.multiple_of((1 - place_ref[1]) * share, 128), wide)
        pairs = [
            (ref.at[units, :] if axis == 0 else ref.at[:, units], out_ref.at[k])
            for k, ref in enumerate((weight_ref, probe_ref))
        ]
        wait_all(run_copies(pairs, sems))

    scratch = [pltpu.SemaphoreType.DMA((2,))]
    return call(kernel, shape(2, *dims), HBM, scratch, (place, weight, probe), [SMEM, HBM, HBM])


def position(block_of, z, core):
    delta = lax.rem((1 - 2 * core) * (block_of - z) + 16, 8)
    return jnp.where(delta == 0, 0, jnp.where(delta <= 3, 2 * delta, 15 - 2 * delta))


def assemble(place, plane, other):
    rows, width = plane.shape[1:]

    def kernel(plane_ref, other_ref, out_ref):
        for j in range(8):
            for far in range(2):
                chip = (j % 4) * 4 + 2 * (j // 4) + far
                cols = slice(far * width, (far + 1) * width)
                for src, first in ((plane_ref, 0), (other_ref, 8)):
                    out_ref[(first + j) * rows : (first + j + 1) * rows, cols] = src[chip]

    return call(kernel, shape(16 * rows, 2 * width), VMEM, [], (plane, other), [VMEM, VMEM])


def to_own_order(src_ref, dst_ref, place_ref):
    rows = src_ref.shape[0] // 8
    for b in range(8):
        spot = pl.multiple_of(position(b, place_ref[0], place_ref[2]) * rows, 16)
        dst_ref[pl.ds(spot, rows), :] = src_ref[b * rows : (b + 1) * rows, :]


def contract(one, two, one_dim, two_dim):
    return lax.dot_general(one, two, (((one_dim,), (two_dim,)), ((), ())), preferred_element_type=F32)


def product(place, rows_in, weight, probe, far, axis):
    tokens, features = rows_in.shape[0], rows_in.shape[1] // 2
    share = weight.shape[axis] // 2
    wide, narrow = widths(share)
    dims = lambda units: (2, units, features) if axis == 0 else (2, features, units)

    def kernel(place_ref, rows_ref, weight_ref, probe_ref, far_ref, out_ref, mine, theirs, rows, sems):
        half = place_ref[1]
        first = pl.ds(pl.multiple_of(half * share, 128), share)
        second = pl.ds(pl.multiple_of((1 - half) * share + wide, 128), narrow)
        pairs = []
        for k, ref in enumerate((weight_ref, probe_ref)):
            for units, dst in ((first, mine), (second, theirs)):
                pairs.append((ref.at[units, :] if axis == 0 else ref.at[:, units], dst.at[k]))
        copies = run_copies(pairs, sems)
        to_own_order(rows_ref, rows, place_ref)
        wait_all(copies)
        own = rows[:, :features]
        for k in range(2):
            if axis == 0:
                parts = (mine[k, :wide], mine[k, wide:], theirs[k])
            else:
                parts = (mine[k, :, :wide], mine[k, :, wide:], theirs[k])
            one, two, three = (contract(own, part, 1, 1 - axis) for part in parts)
            one += contract(rows[:, features:], far_ref[k], 1, 1 - axis)
            out_ref[:, k * wide : (k + 1) * wide] = one.astype(BF16)
            start = 2 * wide + k * narrow
            out_ref[:, start : start + narrow] = two.astype(BF16)
            out_ref[:, start + 2 * narrow : start + 3 * narrow] = three.astype(BF16)

    scratch = [
        pltpu.VMEM(dims(share), BF16),
        pltpu.VMEM(dims(narrow), BF16),
        pltpu.VMEM(rows_in.shape, BF16),
        pltpu.SemaphoreType.DMA((4,)),
    ]
    args = (place, rows_in, weight, probe, far)
    return call(kernel, shape(tokens, 2 * wide + 4 * narrow), VMEM, scratch, args, [SMEM, VMEM, HBM, HBM, VMEM])


def stack_blocks(refs, start, dst_ref):
    rows, width = dst_ref.shape[0] // 8, dst_ref.shape[1]
    for p, ref in enumerate(refs):
        dst_ref[p * rows : (p + 1) * rows, :] = ref[:, start : start + width]


def put(pairs, sems):
    wait_all(run_copies(pairs, sems))


def wide_gradients(place, rows_in, blocks, start, probe, far, axis):
    features = rows_in.shape[1] // 2
    share = probe.shape[axis] // 2
    wide, _ = widths(share)
    count = len(blocks)
    dims = (wide, features) if axis == 0 else (features, wide)

    def kernel(place_ref, rows_ref, probe_ref, far_ref, *rest):
        refs, (grad_out, hess_out, sent_ref, rows, acts, own, kept, sems) = rest[:count], rest[count:]
        units = pl.ds(pl.multiple_of(place_ref[1] * share, 128), wide)
        at = lambda ref: ref.at[units, :] if axis == 0 else ref.at[:, units]
        copies = run_copies([(at(probe_ref), own)], sems)
        to_own_order(rows_ref, rows, place_ref)
        stack_blocks(refs, start, acts)
        wait_all(copies)

        def fill(dst, block_rows, block_probe):
            if axis == 0:
                total = contract(acts[...], block_rows, 0, 0)
                grad, hess = total[:wide], total[wide:]
            else:
                total = contract(block_rows, acts[...], 0, 0)
                grad, hess = total[:, :wide], total[:, wide:]
            dst[0] = grad.astype(BF16)
            dst[1] = (block_probe.astype(F32) * hess).astype(BF16)

        fill(sent_ref, rows[:, features:], far_ref[1])
        fill(kept, rows[:, :features], own[...])
        put([(kept.at[k], at(ref)) for k, ref in enumerate((grad_out, hess_out))], sems)

    whole = shape(*probe.shape)
    scratch = [
        pltpu.VMEM(rows_in.shape, BF16),
        pltpu.VMEM((rows_in.shape[0], 2 * wide), BF16),
        pltpu.VMEM(dims, BF16),
        pltpu.VMEM((2, *dims), BF16),
        pltpu.SemaphoreType.DMA((2,)),
    ]
    args = (place, rows_in, probe, far, *blocks)
    specs = [SMEM, VMEM, HBM, VMEM] + [VMEM] * count
    return call(kernel, [whole, whole, shape(2, *dims)], [HBM, HBM, VMEM], scratch, args, specs)


def narrow_gradients(place, rows_in, blocks, start, probe, axis, outs):
    features = rows_in.shape[1] // 2
    share = probe.shape[axis] // 2
    wide, narrow = widths(share)
    count = len(blocks)
    dims = (narrow, features) if axis == 0 else (features, narrow)
    skip = blocks[0].shape[1] // 2

    def kernel(place_ref, rows_ref, probe_ref, *rest):
        refs, (grad_out, hess_out, rows, acts, own, kept, sems) = rest[:count], rest[count + 2 :]
        half = place_ref[1]
        places = [pl.ds(pl.multiple_of(h * share + wide, 128), narrow) for h in (half, 1 - half)]
        at = lambda ref, units: ref.at[units, :] if axis == 0 else ref.at[:, units]
        copies = run_copies([(at(probe_ref, units), own.at[i]) for i, units in enumerate(places)], sems)
        to_own_order(rows_ref, rows, place_ref)
        for i in range(2):
            stack_blocks(refs, start + i * skip, acts.at[i])
        wait_all(copies)
        for i in range(2):
            if axis == 0:
                total = contract(acts[i], rows[:, :features], 0, 0)
                grad, hess = total[:narrow], total[narrow:]
            else:
                total = contract(rows[:, :features], acts[i], 0, 0)
                grad, hess = total[:, :narrow], total[:, narrow:]
            kept[2 * i] = grad.astype(BF16)
            kept[2 * i + 1] = (own[i].astype(F32) * hess).astype(BF16)
        put([(kept.at[2 * i + k], at(ref, places[i])) for i in range(2) for k, ref in enumerate((grad_out, hess_out))], sems)

    whole = shape(*probe.shape)
    scratch = [
        pltpu.VMEM(rows_in.shape, BF16),
        pltpu.VMEM((2, rows_in.shape[0], 2 * narrow), BF16),
        pltpu.VMEM((2, *dims), BF16),
        pltpu.VMEM((4, *dims), BF16),
        pltpu.SemaphoreType.DMA((4,)),
    ]
    args = (place, rows_in, probe, *blocks, *outs)
    specs = [SMEM, VMEM, HBM] + [VMEM] * count + [HBM] * 2
    return call(kernel, [whole, whole], [HBM, HBM], scratch, args, specs, {3 + count: 0, 4 + count: 1})


def place_taken(place, taken, outs, axis):
    share = outs[0].shape[axis] // 2
    wide, _ = widths(share)

    def kernel(place_ref, taken_ref, *rest):
        refs, sems = rest[2:4], rest[4]
        units = pl.ds(pl.multiple_of((1 - place_ref[1]) * share, 128), wide)
        put([(taken_ref.at[k], ref.at[units, :] if axis == 0 else ref.at[:, units]) for k, ref in enumerate(refs)], sems)

    args = (place, taken, *outs)
    scratch = [pltpu.SemaphoreType.DMA((2,))]
    return call(kernel, [shape(*o.shape) for o in outs], [HBM] * 2, scratch, args, [SMEM] + [HBM] * 3, {2: 0, 3: 1})


def part_at(rows, step):
    count = rows.shape[0] // 8
    return lax.slice_in_dim(rows, ORDER.index(step) * count, (ORDER.index(step) + 1) * count, axis=0)


def reduce_z(part, gates=()):
    main, minor = part_at(part, -4), part_at(part, -3)
    marks = []
    for step in range(4):
        if step < len(gates) and gates[step] is not None:
            main, minor = after((main, minor), gates[step])
        main = send(main, MAIN)
        if step < 3:
            minor = send(minor, MINOR)
        marks.append((main, minor))
        if step < 3:
            main = add(main, part_at(part, 3 - step))
        if step < 2:
            minor = add(minor, part_at(part, step - 2))
    return main.astype(F32) + minor.astype(F32) + part_at(part, 0).astype(F32), marks


def gather_z(part):
    out, main, minor = [part], part, part
    for step in range(4):
        main = send(main, MAIN)
        out.append(main)
        if step < 3:
            minor = send(minor, MINOR)
            out.append(minor)
    return out


def normalize(tok, full_width, event):
    values = tok.astype(F32)
    sums = jnp.stack([jnp.sum(values, axis=1), jnp.sum(values * values, axis=1)])
    for i, pairs in enumerate(DOUBLING):
        if i == len(DOUBLING) - 1:
            sums = after(sums, event)
        sums = sums + send(sums, pairs)
    mean = (sums[0] / full_width)[:, None]
    scale = lax.rsqrt((sums[1] / full_width)[:, None] - mean * mean + epsilon)
    return ((values - mean) * scale).astype(BF16)


def slopes(forward):
    width = forward.shape[1] // 2
    pre_act, tangent = forward[:, :width], forward[:, width:]
    cumulative = 0.5 * (1.0 + lax.erf(pre_act * inv_root_two))
    density = jnp.exp(-0.5 * pre_act * pre_act) * inv_root_tau
    slope = cumulative + pre_act * density
    curve = density * (2.0 - pre_act * pre_act)
    return pre_act, tangent, cumulative, slope, curve


def hidden_parts(forward):
    pre_act, tangent, cumulative, slope, _ = slopes(forward)
    return jnp.concatenate([(pre_act * cumulative).astype(BF16), (slope * tangent).astype(BF16)], axis=1)


def gradient_parts(forward, backward):
    _, tangent, _, slope, curve = slopes(forward)
    back_grad, tangent_back = jnp.split(backward, 2, axis=1)
    grad_pre = (back_grad * slope).astype(BF16)
    tangent_pre = (tangent_back * slope + back_grad * curve * tangent).astype(BF16)
    return jnp.concatenate([grad_pre, tangent_pre], axis=1)


def after(value, event):
    return lax.optimization_barrier((value, event))[0]


def meet(total, wide, narrow):
    own, theirs = total[:, 2 * wide : 2 * wide + 2 * narrow], total[:, 2 * wide + 2 * narrow :]
    return total[:, : 2 * wide], own, send(theirs.astype(BF16), PARTNER)


def all_parts(forward, backward):
    return jnp.concatenate([gradient_parts(forward, backward), hidden_parts(forward)], axis=1)


def on_device(tokens, cotangent, up_weight, up_probe, down_weight, down_probe):
    full_width = tokens.shape[1] * lax.axis_size("fsdp")
    fsdp = lax.axis_index("fsdp")
    core = lax.axis_index("tensor") % 2
    place = jnp.stack([fsdp // 2, fsdp % 2, core]).astype(jnp.int32)
    wide, narrow = widths(up_weight.shape[1] // 2)

    rows = jnp.stack([tokens, cotangent])
    down_far = send(pack(place, down_weight, down_probe, 0), PARTNER)
    line = jnp.stack([rows] + [send(rows, pairs) for pairs in FIRST])
    up_far = send(after(pack(place, up_weight, up_probe, 1), line), PARTNER)
    plane = jnp.stack([line] + [send(line, pairs) for pairs in SECOND])
    plane = plane.reshape(16, *rows.shape)
    tok, cot = plane[:, 0], plane[:, 1]
    cot, down_far = lax.optimization_barrier((cot, down_far))
    cot = assemble(place, cot, send(cot, CORES))
    part = product(place, cot, down_weight, down_probe, down_far, 0)
    backward, clock = reduce_z(part)
    other = jnp.concatenate([send(half, CORES) for half in jnp.split(tok, 2)])
    tok = assemble(place, tok, other)
    normed = normalize(tok, full_width, up_far)
    part = product(place, after(normed, clock[1]), up_weight, up_probe, up_far, 1)
    forward, _ = reduce_z(part)
    backward_wide, backward_narrow, backward_taken = meet(backward, wide, narrow)
    forward_wide, forward_narrow, forward_taken = meet(forward, wide, narrow)

    blocks = gather_z(all_parts(forward_wide, backward_wide))
    forward_taken = after(forward_taken, blocks[1])
    mine = all_parts(forward_narrow + forward_taken.astype(F32), backward_narrow + backward_taken.astype(F32))
    both = jnp.concatenate([mine, send(mine, PARTNER)], axis=1)
    *up_outs, up_sent = wide_gradients(place, normed, blocks, 0, up_probe, up_far, 1)
    *down_outs, down_sent = wide_gradients(place, cot, blocks, 2 * wide, down_probe, down_far, 0)
    blocks = gather_z(after(both, blocks[3]))
    down_outs = place_taken(place, send(down_sent, PARTNER), down_outs, 0)
    up_taken = send(up_sent, PARTNER)
    down_outs = narrow_gradients(place, cot, blocks, 2 * narrow, down_probe, 0, down_outs)
    up_outs = narrow_gradients(place, normed, blocks, 0, up_probe, 1, up_outs)
    up_outs = place_taken(place, up_taken, up_outs, 1)
    return (*up_outs, *down_outs)


def solution(mesh):
    in_specs = (
        P("tensor", "fsdp"),
        P("tensor", "fsdp"),
        P("fsdp", "tensor"),
        P("fsdp", "tensor"),
        P("tensor", "fsdp"),
        P("tensor", "fsdp"),
    )
    out_specs = (P("fsdp", "tensor"), P("fsdp", "tensor"), P("tensor", "fsdp"), P("tensor", "fsdp"))
    return jax.shard_map(
        on_device, mesh=mesh, in_specs=in_specs, out_specs=out_specs, check_vma=False
    )
```

```python
import jax
import jax.numpy as jnp
from jax import lax
from jax.experimental import pallas as pl
from jax.experimental.pallas import tpu as pltpu
from jax.sharding import PartitionSpec as P

epsilon = 1e-05
inv_root_two = 0.7071067811865476
inv_root_tau = 0.3989422804014327

BOTH = ("fsdp", "tensor")
F32 = jnp.float32
BF16 = jnp.bfloat16


def pairs_of(move):
    pairs = []
    for fsdp in range(16):
        for tensor in range(16):
            x, y, z, core = (tensor // 8) * 2 + fsdp % 2, (tensor // 2) % 4, fsdp // 2, tensor % 2
            x, y, z, core = move(x, y, z, core)
            target = (z % 8 * 2 + x % 2) * 16 + (x // 2) * 8 + y * 2 + core
            pairs.append((fsdp * 16 + tensor, target))
    return pairs


MAIN = pairs_of(lambda x, y, z, c: (x, y, z + 1 - 2 * c, c))
MINOR = pairs_of(lambda x, y, z, c: (x, y, z - 1 + 2 * c, c))
PARTNER = pairs_of(lambda x, y, z, c: (x ^ 1, y, z, c))
CORES = pairs_of(lambda x, y, z, c: (x, y, z, c ^ 1))
FIRST = [pairs_of(lambda x, y, z, c, k=k: (x ^ k, y, z, c)) for k in (1, 2, 3)]
SECOND = [pairs_of(lambda x, y, z, c, k=k: (x, y ^ k, z, c)) for k in (1, 2, 3)]
DOUBLING = [pairs_of(lambda x, y, z, c, k=k: (x, y, z ^ k, c)) for k in (1, 2)]
DOUBLING.append(pairs_of(lambda x, y, z, c: (x, y, z + (2 if z % 4 > 1 else -2) + 8, c)))


def send(value, pairs):
    return lax.ppermute(value, BOTH, pairs)


def add(one, two):
    return (one.astype(F32) + two.astype(F32)).astype(BF16)


ORDER = (0, -1, 1, -2, 2, -3, 3, -4)
HBM = pl.BlockSpec(memory_space=pltpu.HBM)
VMEM = pl.BlockSpec(memory_space=pltpu.VMEM)
SMEM = pl.BlockSpec(memory_space=pltpu.SMEM)


def call(kernel, outs, out_specs, scratch, args, specs, aliases=None, flops=0):
    return pl.pallas_call(
        kernel,
        out_shape=outs,
        in_specs=specs,
        out_specs=out_specs,
        scratch_shapes=scratch,
        input_output_aliases=aliases or {},
        compiler_params=pltpu.CompilerParams(vmem_limit_bytes=40 * 2**20),
        cost_estimate=pl.CostEstimate(flops=flops, bytes_accessed=1024, transcendentals=0),
    )(*args)


def shape(*dims, dtype=BF16):
    return jax.ShapeDtypeStruct(dims, dtype)


def run_copies(pairs, sems):
    copies = [pltpu.make_async_copy(src, dst, sems.at[i]) for i, (src, dst) in enumerate(pairs)]
    for copy in copies:
        copy.start()
    return copies


def wait_all(copies):
    for copy in copies:
        copy.wait()


def after(value, event):
    return lax.optimization_barrier((value, event))[0]


def widths(share):
    return share * 2 // 3, share - share * 2 // 3


def pack(place, weight, probe, axis):
    share = weight.shape[axis] // 2
    wide, _ = widths(share)
    dims = (wide, weight.shape[1]) if axis == 0 else (weight.shape[0], wide)

    def kernel(place_ref, weight_ref, probe_ref, out_ref, sems):
        units = pl.ds(pl.multiple_of((1 - place_ref[1]) * share, 128), wide)
        pairs = [
            (ref.at[units, :] if axis == 0 else ref.at[:, units], out_ref.at[k])
            for k, ref in enumerate((weight_ref, probe_ref))
        ]
        wait_all(run_copies(pairs, sems))

    scratch = [pltpu.SemaphoreType.DMA((2,))]
    return call(kernel, shape(2, *dims), HBM, scratch, (place, weight, probe), [SMEM, HBM, HBM])


def position(block_of, z, core):
    delta = lax.rem((1 - 2 * core) * (block_of - z) + 16, 8)
    return jnp.where(delta == 0, 0, jnp.where(delta <= 3, 2 * delta, 15 - 2 * delta))


def assemble(place, plane, other):
    rows, width = plane.shape[1:]

    def kernel(plane_ref, other_ref, out_ref):
        for j in range(8):
            for far in range(2):
                chip = (j % 4) * 4 + 2 * (j // 4) + far
                cols = slice(far * width, (far + 1) * width)
                for src, first in ((plane_ref, 0), (other_ref, 8)):
                    out_ref[(first + j) * rows : (first + j + 1) * rows, cols] = src[chip]

    return call(kernel, shape(16 * rows, 2 * width), VMEM, [], (plane, other), [VMEM, VMEM])


def to_own_order(src_ref, dst_ref, place_ref):
    rows = src_ref.shape[0] // 8
    for b in range(8):
        spot = pl.multiple_of(position(b, place_ref[0], place_ref[2]) * rows, 16)
        dst_ref[pl.ds(spot, rows), :] = src_ref[b * rows : (b + 1) * rows, :]


def contract(one, two, one_dim, two_dim):
    return lax.dot_general(one, two, (((one_dim,), (two_dim,)), ((), ())), preferred_element_type=F32)


def product(place, rows_in, weight, probe, far, axis):
    tokens, features = rows_in.shape[0], rows_in.shape[1] // 2
    share = weight.shape[axis] // 2
    wide, narrow = widths(share)
    dims = lambda units: (2, units, features) if axis == 0 else (2, features, units)

    def kernel(place_ref, rows_ref, weight_ref, probe_ref, far_ref, out_ref, mine, theirs, rows, sems):
        half = place_ref[1]
        first = pl.ds(pl.multiple_of(half * share, 128), share)
        second = pl.ds(pl.multiple_of((1 - half) * share + wide, 128), narrow)
        pairs = []
        for k, ref in enumerate((weight_ref, probe_ref)):
            for units, dst in ((first, mine), (second, theirs)):
                pairs.append((ref.at[units, :] if axis == 0 else ref.at[:, units], dst.at[k]))
        copies = run_copies(pairs, sems)
        to_own_order(rows_ref, rows, place_ref)
        wait_all(copies)
        own = rows[:, :features]
        for k in range(2):
            if axis == 0:
                parts = (mine[k, :wide], mine[k, wide:], theirs[k])
            else:
                parts = (mine[k, :, :wide], mine[k, :, wide:], theirs[k])
            one, two, three = (contract(own, part, 1, 1 - axis) for part in parts)
            one += contract(rows[:, features:], far_ref[k], 1, 1 - axis)
            out_ref[:, k * wide : (k + 1) * wide] = one.astype(BF16)
            start = 2 * wide + k * narrow
            out_ref[:, start : start + narrow] = two.astype(BF16)
            out_ref[:, start + 2 * narrow : start + 3 * narrow] = three.astype(BF16)

    scratch = [
        pltpu.VMEM(dims(share), BF16),
        pltpu.VMEM(dims(narrow), BF16),
        pltpu.VMEM(rows_in.shape, BF16),
        pltpu.SemaphoreType.DMA((4,)),
    ]
    args = (place, rows_in, weight, probe, far)
    return call(kernel, shape(tokens, 2 * wide + 4 * narrow), VMEM, scratch, args, [SMEM, VMEM, HBM, HBM, VMEM])


def stack_blocks(refs, start, dst_ref):
    rows, width = dst_ref.shape[0] // 8, dst_ref.shape[1]
    for p, ref in enumerate(refs):
        dst_ref[p * rows : (p + 1) * rows, :] = ref[:, start : start + width]


def put(pairs, sems):
    wait_all(run_copies(pairs, sems))


def wide_gradients(place, rows_in, blocks, start, probe, far, axis):
    features = rows_in.shape[1] // 2
    share = probe.shape[axis] // 2
    wide, _ = widths(share)
    count = len(blocks)
    dims = (wide, features) if axis == 0 else (features, wide)

    def fill(dst, acts, block_rows, block_probe):
        if axis == 0:
            total = contract(acts[...], block_rows, 0, 0)
            grad, hess = total[:wide], total[wide:]
        else:
            total = contract(block_rows, acts[...], 0, 0)
            grad, hess = total[:, :wide], total[:, wide:]
        dst[0] = grad.astype(BF16)
        dst[1] = (block_probe.astype(F32) * hess).astype(BF16)

    def far_kernel(place_ref, rows_ref, far_ref, *rest):
        refs, (sent_ref, acts, rows) = rest[:count], rest[count:]
        to_own_order(rows_ref, rows, place_ref)
        stack_blocks(refs, start, acts)
        fill(sent_ref, acts, rows[:, features:], far_ref[1])

    def own_kernel(place_ref, rows_ref, probe_ref, acts, grad_out, hess_out, rows, own, kept, sems):
        units = pl.ds(pl.multiple_of(place_ref[1] * share, 128), wide)
        at = lambda ref: ref.at[units, :] if axis == 0 else ref.at[:, units]
        copies = run_copies([(at(probe_ref), own)], sems)
        to_own_order(rows_ref, rows, place_ref)
        wait_all(copies)
        fill(kept, acts, rows[:, :features], own[...])
        put([(kept.at[k], at(ref)) for k, ref in enumerate((grad_out, hess_out))], sems)

    ordered = pltpu.VMEM(rows_in.shape, BF16)
    acts_shape = shape(rows_in.shape[0], 2 * wide)
    specs = [SMEM, VMEM, VMEM] + [VMEM] * count
    sent, acts = call(far_kernel, [shape(2, *dims), acts_shape], [VMEM] * 2, [ordered], (place, rows_in, far, *blocks), specs)

    def own(event):
        whole = shape(*probe.shape)
        scratch = [ordered, pltpu.VMEM(dims, BF16), pltpu.VMEM((2, *dims), BF16), pltpu.SemaphoreType.DMA((2,))]
        args = (place, rows_in, probe, after(acts, event))
        return call(own_kernel, [whole, whole], [HBM, HBM], scratch, args, [SMEM, VMEM, HBM, VMEM])

    return sent, own


def narrow_gradients(place, normed, cot, blocks, up_probe, down_probe, outs):
    tokens, features = normed.shape[0], normed.shape[1] // 2
    share = down_probe.shape[0] // 2
    wide, narrow = widths(share)
    count = len(blocks)

    def kernel(place_ref, normed_ref, cot_ref, up_ref, down_ref, *rest):
        refs, (*out_refs, up_rows, down_rows, acts, up_own, down_own, up_kept, down_kept, sems) = rest[:count], rest[count + 4 :]
        half = place_ref[1]
        places = [pl.ds(pl.multiple_of(h * share + wide, 128), narrow) for h in (half, 1 - half)]
        probes = [(up_ref.at[:, units], up_own.at[i]) for i, units in enumerate(places)]
        probes += [(down_ref.at[units, :], down_own.at[i]) for i, units in enumerate(places)]
        copies = run_copies(probes, sems)
        to_own_order(normed_ref, up_rows, place_ref)
        to_own_order(cot_ref, down_rows, place_ref)
        stack_blocks(refs, 0, acts)
        wait_all(copies)
        copies = []
        for i, units in enumerate(places):
            start = i * 4 * narrow
            total = contract(up_rows[:, :features], acts[:, start : start + 2 * narrow], 0, 0)
            up_kept[2 * i] = total[:, :narrow].astype(BF16)
            up_kept[2 * i + 1] = (up_own[i].astype(F32) * total[:, narrow:]).astype(BF16)
            for k in range(2):
                copies.append(pltpu.make_async_copy(up_kept.at[2 * i + k], out_refs[k].at[:, units], sems.at[4 * i + k]))
                copies[-1].start()
            total = contract(acts[:, start + 2 * narrow : start + 4 * narrow], down_rows[:, :features], 0, 0)
            down_kept[2 * i] = total[:narrow].astype(BF16)
            down_kept[2 * i + 1] = (down_own[i].astype(F32) * total[narrow:]).astype(BF16)
            for k in range(2):
                copies.append(pltpu.make_async_copy(down_kept.at[2 * i + k], out_refs[2 + k].at[units, :], sems.at[4 * i + 2 + k]))
                copies[-1].start()
        wait_all(copies)

    scratch = [
        pltpu.VMEM(normed.shape, BF16),
        pltpu.VMEM(cot.shape, BF16),
        pltpu.VMEM((tokens, 8 * narrow), BF16),
        pltpu.VMEM((2, features, narrow), BF16),
        pltpu.VMEM((2, narrow, features), BF16),
        pltpu.VMEM((4, features, narrow), BF16),
        pltpu.VMEM((4, narrow, features), BF16),
        pltpu.SemaphoreType.DMA((8,)),
    ]
    args = (place, normed, cot, up_probe, down_probe, *blocks, *outs)
    specs = [SMEM, VMEM, VMEM, HBM, HBM] + [VMEM] * count + [HBM] * 4
    aliases = {5 + count + k: k for k in range(4)}
    return call(kernel, [shape(*o.shape) for o in outs], [HBM] * 4, scratch, args, specs, aliases)


def place_taken(place, taken, outs, axis):
    share = outs[0].shape[axis] // 2
    wide, _ = widths(share)

    def kernel(place_ref, taken_ref, *rest):
        refs, sems = rest[2:4], rest[4]
        units = pl.ds(pl.multiple_of((1 - place_ref[1]) * share, 128), wide)
        put([(taken_ref.at[k], ref.at[units, :] if axis == 0 else ref.at[:, units]) for k, ref in enumerate(refs)], sems)

    args = (place, taken, *outs)
    scratch = [pltpu.SemaphoreType.DMA((2,))]
    return call(kernel, [shape(*o.shape) for o in outs], [HBM] * 2, scratch, args, [SMEM] + [HBM] * 3, {2: 0, 3: 1})


def part_at(rows, step):
    count = rows.shape[0] // 8
    return lax.slice_in_dim(rows, ORDER.index(step) * count, (ORDER.index(step) + 1) * count, axis=0)


def reduce_z(part, gates=()):
    main, minor = part_at(part, -4), part_at(part, -3)
    marks = []
    for step in range(4):
        if step < len(gates) and gates[step] is not None:
            main, minor = after((main, minor), gates[step])
        main = send(main, MAIN)
        if step < 3:
            minor = send(minor, MINOR)
        marks.append((main, minor))
        if step < 3:
            main = add(main, part_at(part, 3 - step))
        if step < 2:
            minor = add(minor, part_at(part, step - 2))
    return main.astype(F32) + minor.astype(F32) + part_at(part, 0).astype(F32), marks


def gather_z(part):
    out, main, minor = [part], part, part
    for step in range(4):
        main = send(main, MAIN)
        out.append(main)
        if step < 3:
            minor = send(minor, MINOR)
            out.append(minor)
    return out


def normalize(tok, full_width, events):
    values = tok.astype(F32)
    sums = jnp.stack([jnp.sum(values, axis=1), jnp.sum(values * values, axis=1)])
    for i, pairs in enumerate(DOUBLING):
        if events[i] is not None:
            sums = after(sums, events[i])
        sums = sums + send(sums, pairs)
    mean = (sums[0] / full_width)[:, None]
    scale = lax.rsqrt((sums[1] / full_width)[:, None] - mean * mean + epsilon)
    return ((values - mean) * scale).astype(BF16)


def slopes(forward):
    width = forward.shape[1] // 2
    pre_act, tangent = forward[:, :width], forward[:, width:]
    cumulative = 0.5 * (1.0 + lax.erf(pre_act * inv_root_two))
    density = jnp.exp(-0.5 * pre_act * pre_act) * inv_root_tau
    slope = cumulative + pre_act * density
    curve = density * (2.0 - pre_act * pre_act)
    return pre_act, tangent, cumulative, slope, curve


def hidden_parts(forward):
    pre_act, tangent, cumulative, slope, _ = slopes(forward)
    return jnp.concatenate([(pre_act * cumulative).astype(BF16), (slope * tangent).astype(BF16)], axis=1)


def gradient_parts(forward, backward):
    _, tangent, _, slope, curve = slopes(forward)
    back_grad, tangent_back = jnp.split(backward, 2, axis=1)
    grad_pre = (back_grad * slope).astype(BF16)
    tangent_pre = (tangent_back * slope + back_grad * curve * tangent).astype(BF16)
    return jnp.concatenate([grad_pre, tangent_pre], axis=1)


def meet(total, wide, narrow):
    own, theirs = total[:, 2 * wide : 2 * wide + 2 * narrow], total[:, 2 * wide + 2 * narrow :]
    return total[:, : 2 * wide], own, send(theirs.astype(BF16), PARTNER)


def all_parts(forward, backward):
    return jnp.concatenate([gradient_parts(forward, backward), hidden_parts(forward)], axis=1)


def on_device(tokens, cotangent, up_weight, up_probe, down_weight, down_probe):
    full_width = tokens.shape[1] * lax.axis_size("fsdp")
    fsdp = lax.axis_index("fsdp")
    core = lax.axis_index("tensor") % 2
    place = jnp.stack([fsdp // 2, fsdp % 2, core]).astype(jnp.int32)
    wide, narrow = widths(up_weight.shape[1] // 2)

    rows = jnp.stack([tokens, cotangent])
    packed = pack(place, down_weight, down_probe, 0)
    line = jnp.stack([rows] + [send(rows, pairs) for pairs in FIRST])
    line, packed = lax.optimization_barrier((line, packed))
    down_far = send(packed, PARTNER)
    packed = pack(place, up_weight, up_probe, 1)
    plane = jnp.stack([line] + [send(line, pairs) for pairs in SECOND])
    plane = plane.reshape(16, *rows.shape)
    tok, cot = plane[:, 0], plane[:, 1]
    tok, packed = lax.optimization_barrier((tok, packed))
    up_far = send(packed, PARTNER)
    other = jnp.concatenate([send(half, CORES) for half in jnp.split(tok, 2)])
    tok = assemble(place, tok, other)
    cot = after(cot, (other, down_far))
    cot = assemble(place, cot, send(cot, CORES))
    part = product(place, cot, down_weight, down_probe, down_far, 0)
    normed = normalize(tok, full_width, (None, part, up_far))
    backward, _ = reduce_z(after(part, up_far))
    part = product(place, normed, up_weight, up_probe, up_far, 1)
    forward, _ = reduce_z(part)
    backward_wide, backward_narrow, backward_taken = meet(backward, wide, narrow)
    forward_wide, forward_narrow, forward_taken = meet(forward, wide, narrow)

    blocks = gather_z(all_parts(forward_wide, backward_wide))
    forward_taken = after(forward_taken, blocks[1])
    mine = all_parts(forward_narrow + forward_taken.astype(F32), backward_narrow + backward_taken.astype(F32))
    both = jnp.concatenate([mine, send(mine, PARTNER)], axis=1)
    down_sent, down_own = wide_gradients(place, cot, blocks, 2 * wide, down_probe, down_far, 0)
    up_sent, up_own = wide_gradients(place, normed, blocks, 0, up_probe, up_far, 1)
    down_outs, up_outs = down_own(up_sent), up_own(up_sent)
    blocks = gather_z(after(both, blocks[3]))
    down_outs = place_taken(place, send(down_sent, PARTNER), down_outs, 0)
    up_outs = place_taken(place, send(up_sent, PARTNER), up_outs, 1)
    return tuple(narrow_gradients(place, normed, cot, blocks, up_probe, down_probe, (*up_outs, *down_outs)))


def solution(mesh):
    in_specs = (
        P("tensor", "fsdp"),
        P("tensor", "fsdp"),
        P("fsdp", "tensor"),
        P("fsdp", "tensor"),
        P("tensor", "fsdp"),
        P("tensor", "fsdp"),
    )
    out_specs = (P("fsdp", "tensor"), P("fsdp", "tensor"), P("tensor", "fsdp"), P("tensor", "fsdp"))
    return jax.shard_map(
        on_device, mesh=mesh, in_specs=in_specs, out_specs=out_specs, check_vma=False
    )
```

```python
import jax
import jax.numpy as jnp
from jax import lax
from jax.experimental import pallas as pl
from jax.experimental.pallas import tpu as pltpu
from jax.sharding import PartitionSpec as P

epsilon = 1e-05
inv_root_two = 0.7071067811865476
inv_root_tau = 0.3989422804014327

BOTH = ("fsdp", "tensor")
F32 = jnp.float32
BF16 = jnp.bfloat16


def pairs_of(move):
    pairs = []
    for fsdp in range(16):
        for tensor in range(16):
            x, y, z, core = (tensor // 8) * 2 + fsdp % 2, (tensor // 2) % 4, fsdp // 2, tensor % 2
            x, y, z, core = move(x, y, z, core)
            target = (z % 8 * 2 + x % 2) * 16 + (x // 2) * 8 + y * 2 + core
            pairs.append((fsdp * 16 + tensor, target))
    return pairs


MAIN = pairs_of(lambda x, y, z, c: (x, y, z + 1 - 2 * c, c))
MINOR = pairs_of(lambda x, y, z, c: (x, y, z - 1 + 2 * c, c))
PARTNER = pairs_of(lambda x, y, z, c: (x ^ 1, y, z, c))
CORES = pairs_of(lambda x, y, z, c: (x, y, z, c ^ 1))
FIRST = [pairs_of(lambda x, y, z, c, k=k: (x ^ k, y, z, c)) for k in (1, 2, 3)]
SECOND = [pairs_of(lambda x, y, z, c, k=k: (x, y ^ k, z, c)) for k in (1, 2, 3)]
DOUBLING = [pairs_of(lambda x, y, z, c, k=k: (x, y, z ^ k, c)) for k in (1, 2)]
DOUBLING.append(pairs_of(lambda x, y, z, c: (x, y, z + (2 if z % 4 > 1 else -2) + 8, c)))


def send(value, pairs):
    return lax.ppermute(value, BOTH, pairs)


def add(one, two):
    return (one.astype(F32) + two.astype(F32)).astype(BF16)


ORDER = (0, -1, 1, -2, 2, -3, 3, -4)
HBM = pl.BlockSpec(memory_space=pltpu.HBM)
VMEM = pl.BlockSpec(memory_space=pltpu.VMEM)
SMEM = pl.BlockSpec(memory_space=pltpu.SMEM)


def call(kernel, outs, out_specs, scratch, args, specs, aliases=None, flops=0):
    return pl.pallas_call(
        kernel,
        out_shape=outs,
        in_specs=specs,
        out_specs=out_specs,
        scratch_shapes=scratch,
        input_output_aliases=aliases or {},
        compiler_params=pltpu.CompilerParams(vmem_limit_bytes=40 * 2**20),
        cost_estimate=pl.CostEstimate(flops=flops, bytes_accessed=1024, transcendentals=0),
    )(*args)


def shape(*dims, dtype=BF16):
    return jax.ShapeDtypeStruct(dims, dtype)


def run_copies(pairs, sems):
    copies = [pltpu.make_async_copy(src, dst, sems.at[i]) for i, (src, dst) in enumerate(pairs)]
    for copy in copies:
        copy.start()
    return copies


def wait_all(copies):
    for copy in copies:
        copy.wait()


def after(value, event):
    return lax.optimization_barrier((value, event))[0]


def widths(share):
    return share * 2 // 3, share - share * 2 // 3


def pack(place, weight, probe, axis):
    share = weight.shape[axis] // 2
    wide, _ = widths(share)
    dims = (wide, weight.shape[1]) if axis == 0 else (weight.shape[0], wide)

    def kernel(place_ref, weight_ref, probe_ref, out_ref, sems):
        units = pl.ds(pl.multiple_of((1 - place_ref[1]) * share, 128), wide)
        pairs = [
            (ref.at[units, :] if axis == 0 else ref.at[:, units], out_ref.at[k])
            for k, ref in enumerate((weight_ref, probe_ref))
        ]
        wait_all(run_copies(pairs, sems))

    scratch = [pltpu.SemaphoreType.DMA((2,))]
    return call(kernel, shape(2, *dims), HBM, scratch, (place, weight, probe), [SMEM, HBM, HBM])


def position(block_of, z, core):
    delta = lax.rem((1 - 2 * core) * (block_of - z) + 16, 8)
    return jnp.where(delta == 0, 0, jnp.where(delta <= 3, 2 * delta, 15 - 2 * delta))


def assemble(place, plane, other):
    rows, width = plane.shape[1:]

    def kernel(plane_ref, other_ref, out_ref):
        for j in range(8):
            for far in range(2):
                chip = (j % 4) * 4 + 2 * (j // 4) + far
                cols = slice(far * width, (far + 1) * width)
                for src, first in ((plane_ref, 0), (other_ref, 8)):
                    out_ref[(first + j) * rows : (first + j + 1) * rows, cols] = src[chip]

    return call(kernel, shape(16 * rows, 2 * width), VMEM, [], (plane, other), [VMEM, VMEM])


def to_own_order(src_ref, dst_ref, place_ref):
    rows = src_ref.shape[0] // 8
    for b in range(8):
        spot = pl.multiple_of(position(b, place_ref[0], place_ref[2]) * rows, 16)
        dst_ref[pl.ds(spot, rows), :] = src_ref[b * rows : (b + 1) * rows, :]


def contract(one, two, one_dim, two_dim):
    return lax.dot_general(one, two, (((one_dim,), (two_dim,)), ((), ())), preferred_element_type=F32)


def product(place, rows_in, weight, probe, far, axis):
    tokens, features = rows_in.shape[0], rows_in.shape[1] // 2
    share = weight.shape[axis] // 2
    wide, narrow = widths(share)

    def kernel(place_ref, rows_ref, weight_ref, probe_ref, far_ref, out_ref, rows):
        half = place_ref[1]
        starts = ((half * share, wide), (half * share + wide, narrow), ((1 - half) * share + wide, narrow))
        to_own_order(rows_ref, rows, place_ref)
        for k, ref in enumerate((weight_ref, probe_ref)):
            units = [pl.ds(pl.multiple_of(start, 128), count) for start, count in starts]
            parts = [ref[u, :] if axis == 0 else ref[:, u] for u in units]
            one, two, three = (contract(rows[:, :features], part, 1, 1 - axis) for part in parts)
            one += contract(rows[:, features:], far_ref[k], 1, 1 - axis)
            out_ref[:, k * wide : (k + 1) * wide] = one.astype(BF16)
            start = 2 * wide + k * narrow
            out_ref[:, start : start + narrow] = two.astype(BF16)
            out_ref[:, start + 2 * narrow : start + 3 * narrow] = three.astype(BF16)

    args = (place, rows_in, weight, probe, far)
    scratch = [pltpu.VMEM(rows_in.shape, BF16)]
    return call(kernel, shape(tokens, 2 * wide + 4 * narrow), VMEM, scratch, args, [SMEM] + [VMEM] * 4)


def stack_blocks(refs, start, dst_ref):
    rows, width = dst_ref.shape[0] // 8, dst_ref.shape[1]
    for p, ref in enumerate(refs):
        dst_ref[p * rows : (p + 1) * rows, :] = ref[:, start : start + width]


def put(pairs, sems):
    wait_all(run_copies(pairs, sems))


def wide_gradients(place, rows_in, blocks, start, probe, far, axis):
    features = rows_in.shape[1] // 2
    share = probe.shape[axis] // 2
    wide, _ = widths(share)
    count = len(blocks)
    dims = (wide, features) if axis == 0 else (features, wide)

    def fill(dst, acts, block_rows, block_probe):
        if axis == 0:
            total = contract(acts[...], block_rows, 0, 0)
            grad, hess = total[:wide], total[wide:]
        else:
            total = contract(block_rows, acts[...], 0, 0)
            grad, hess = total[:, :wide], total[:, wide:]
        dst[0] = grad.astype(BF16)
        dst[1] = (block_probe.astype(F32) * hess).astype(BF16)

    def far_kernel(place_ref, rows_ref, far_ref, *rest):
        refs, (sent_ref, acts, rows) = rest[:count], rest[count:]
        to_own_order(rows_ref, rows, place_ref)
        stack_blocks(refs, start, acts)
        fill(sent_ref, acts, rows[:, features:], far_ref[1])

    def own_kernel(place_ref, rows_ref, probe_ref, acts, grad_out, hess_out, rows, own, kept, sems):
        units = pl.ds(pl.multiple_of(place_ref[1] * share, 128), wide)
        at = lambda ref: ref.at[units, :] if axis == 0 else ref.at[:, units]
        copies = run_copies([(at(probe_ref), own)], sems)
        to_own_order(rows_ref, rows, place_ref)
        wait_all(copies)
        fill(kept, acts, rows[:, :features], own[...])
        put([(kept.at[k], at(ref)) for k, ref in enumerate((grad_out, hess_out))], sems)

    ordered = pltpu.VMEM(rows_in.shape, BF16)
    acts_shape = shape(rows_in.shape[0], 2 * wide)
    specs = [SMEM, VMEM, VMEM] + [VMEM] * count
    sent, acts = call(far_kernel, [shape(2, *dims), acts_shape], [VMEM] * 2, [ordered], (place, rows_in, far, *blocks), specs)

    def own(event):
        whole = shape(*probe.shape)
        scratch = [ordered, pltpu.VMEM(dims, BF16), pltpu.VMEM((2, *dims), BF16), pltpu.SemaphoreType.DMA((2,))]
        args = (place, rows_in, probe, after(acts, event))
        return call(own_kernel, [whole, whole], [HBM, HBM], scratch, args, [SMEM, VMEM, HBM, VMEM])

    return sent, own


def narrow_gradients(place, normed, cot, blocks, up_probe, down_probe, taken, outs):
    tokens, features = normed.shape[0], normed.shape[1] // 2
    share = down_probe.shape[0] // 2
    wide, narrow = widths(share)
    count = len(blocks)

    def kernel(place_ref, normed_ref, cot_ref, up_ref, down_ref, taken_ref, *rest):
        refs, (*out_refs, up_rows, down_rows, acts, up_own, down_own, up_kept, down_kept, sems) = rest[:count], rest[count + 4 :]
        half = place_ref[1]
        places = [pl.ds(pl.multiple_of(h * share + wide, 128), narrow) for h in (half, 1 - half)]
        probes = [(up_ref.at[:, units], up_own.at[i]) for i, units in enumerate(places)]
        probes += [(down_ref.at[units, :], down_own.at[i]) for i, units in enumerate(places)]
        copies = run_copies(probes, sems)
        units = pl.ds(pl.multiple_of((1 - half) * share, 128), wide)
        puts = [pltpu.make_async_copy(taken_ref.at[k], out_refs[k].at[:, units], sems.at[8 + k]) for k in range(2)]
        for copy in puts:
            copy.start()
        to_own_order(normed_ref, up_rows, place_ref)
        to_own_order(cot_ref, down_rows, place_ref)
        stack_blocks(refs, 0, acts)
        wait_all(copies)
        copies = []
        for i, units in enumerate(places):
            start = i * 4 * narrow
            total = contract(up_rows[:, :features], acts[:, start : start + 2 * narrow], 0, 0)
            up_kept[2 * i] = total[:, :narrow].astype(BF16)
            up_kept[2 * i + 1] = (up_own[i].astype(F32) * total[:, narrow:]).astype(BF16)
            for k in range(2):
                copies.append(pltpu.make_async_copy(up_kept.at[2 * i + k], out_refs[k].at[:, units], sems.at[4 * i + k]))
                copies[-1].start()
            total = contract(acts[:, start + 2 * narrow : start + 4 * narrow], down_rows[:, :features], 0, 0)
            down_kept[2 * i] = total[:narrow].astype(BF16)
            down_kept[2 * i + 1] = (down_own[i].astype(F32) * total[narrow:]).astype(BF16)
            for k in range(2):
                copies.append(pltpu.make_async_copy(down_kept.at[2 * i + k], out_refs[2 + k].at[units, :], sems.at[4 * i + 2 + k]))
                copies[-1].start()
        wait_all(copies + puts)

    scratch = [
        pltpu.VMEM(normed.shape, BF16),
        pltpu.VMEM(cot.shape, BF16),
        pltpu.VMEM((tokens, 8 * narrow), BF16),
        pltpu.VMEM((2, features, narrow), BF16),
        pltpu.VMEM((2, narrow, features), BF16),
        pltpu.VMEM((4, features, narrow), BF16),
        pltpu.VMEM((4, narrow, features), BF16),
        pltpu.SemaphoreType.DMA((10,)),
    ]
    args = (place, normed, cot, up_probe, down_probe, taken, *blocks, *outs)
    specs = [SMEM, VMEM, VMEM, HBM, HBM, HBM] + [VMEM] * count + [HBM] * 4
    aliases = {6 + count + k: k for k in range(4)}
    return call(kernel, [shape(*o.shape) for o in outs], [HBM] * 4, scratch, args, specs, aliases)


def place_taken(place, taken, outs, axis):
    share = outs[0].shape[axis] // 2
    wide, _ = widths(share)

    def kernel(place_ref, taken_ref, *rest):
        refs, sems = rest[2:4], rest[4]
        units = pl.ds(pl.multiple_of((1 - place_ref[1]) * share, 128), wide)
        put([(taken_ref.at[k], ref.at[units, :] if axis == 0 else ref.at[:, units]) for k, ref in enumerate(refs)], sems)

    args = (place, taken, *outs)
    scratch = [pltpu.SemaphoreType.DMA((2,))]
    return call(kernel, [shape(*o.shape) for o in outs], [HBM] * 2, scratch, args, [SMEM] + [HBM] * 3, {2: 0, 3: 1})


def part_at(rows, step):
    count = rows.shape[0] // 8
    return lax.slice_in_dim(rows, ORDER.index(step) * count, (ORDER.index(step) + 1) * count, axis=0)


def reduce_z(part, gates=()):
    main, minor = part_at(part, -4), part_at(part, -3)
    marks = []
    for step in range(4):
        if step < len(gates) and gates[step] is not None:
            main, minor = after((main, minor), gates[step])
        main = send(main, MAIN)
        if step < 3:
            minor = send(minor, MINOR)
        marks.append((main, minor))
        if step < 3:
            main = add(main, part_at(part, 3 - step))
        if step < 2:
            minor = add(minor, part_at(part, step - 2))
    return main.astype(F32) + minor.astype(F32) + part_at(part, 0).astype(F32), marks


def gather_z(part):
    out, main, minor = [part], part, part
    for step in range(4):
        main = send(main, MAIN)
        out.append(main)
        if step < 3:
            minor = send(minor, MINOR)
            out.append(minor)
    return out


def normalize(tok, full_width, events):
    values = tok.astype(F32)
    sums = jnp.stack([jnp.sum(values, axis=1), jnp.sum(values * values, axis=1)])
    for i, pairs in enumerate(DOUBLING):
        if events[i] is not None:
            sums = after(sums, events[i])
        sums = sums + send(sums, pairs)
    mean = (sums[0] / full_width)[:, None]
    scale = lax.rsqrt((sums[1] / full_width)[:, None] - mean * mean + epsilon)
    return ((values - mean) * scale).astype(BF16)


def slopes(forward):
    width = forward.shape[1] // 2
    pre_act, tangent = forward[:, :width], forward[:, width:]
    cumulative = 0.5 * (1.0 + lax.erf(pre_act * inv_root_two))
    density = jnp.exp(-0.5 * pre_act * pre_act) * inv_root_tau
    slope = cumulative + pre_act * density
    curve = density * (2.0 - pre_act * pre_act)
    return pre_act, tangent, cumulative, slope, curve


def hidden_parts(forward):
    pre_act, tangent, cumulative, slope, _ = slopes(forward)
    return jnp.concatenate([(pre_act * cumulative).astype(BF16), (slope * tangent).astype(BF16)], axis=1)


def gradient_parts(forward, backward):
    _, tangent, _, slope, curve = slopes(forward)
    back_grad, tangent_back = jnp.split(backward, 2, axis=1)
    grad_pre = (back_grad * slope).astype(BF16)
    tangent_pre = (tangent_back * slope + back_grad * curve * tangent).astype(BF16)
    return jnp.concatenate([grad_pre, tangent_pre], axis=1)


def meet(total, wide, narrow):
    own, theirs = total[:, 2 * wide : 2 * wide + 2 * narrow], total[:, 2 * wide + 2 * narrow :]
    return total[:, : 2 * wide], own, send(theirs.astype(BF16), PARTNER)


def all_parts(forward, backward):
    return jnp.concatenate([gradient_parts(forward, backward), hidden_parts(forward)], axis=1)


def on_device(tokens, cotangent, up_weight, up_probe, down_weight, down_probe):
    full_width = tokens.shape[1] * lax.axis_size("fsdp")
    fsdp = lax.axis_index("fsdp")
    core = lax.axis_index("tensor") % 2
    place = jnp.stack([fsdp // 2, fsdp % 2, core]).astype(jnp.int32)
    wide, narrow = widths(up_weight.shape[1] // 2)

    rows = jnp.stack([tokens, cotangent])
    packed = pack(place, down_weight, down_probe, 0)
    line = jnp.stack([rows] + [send(rows, pairs) for pairs in FIRST])
    line, packed = lax.optimization_barrier((line, packed))
    down_far = send(packed, PARTNER)
    packed = pack(place, up_weight, up_probe, 1)
    plane = jnp.stack([line] + [send(line, pairs) for pairs in SECOND])
    plane = plane.reshape(16, *rows.shape)
    tok, cot = plane[:, 0], plane[:, 1]
    tok, packed = lax.optimization_barrier((tok, packed))
    up_far = send(packed, PARTNER)
    other = jnp.concatenate([send(half, CORES) for half in jnp.split(tok, 2)])
    tok = assemble(place, tok, other)
    cot = after(cot, (other, down_far))
    cot = assemble(place, cot, send(cot, CORES))
    part = product(place, cot, down_weight, down_probe, down_far, 0)
    normed = normalize(tok, full_width, (None, part, up_far))
    backward, _ = reduce_z(after(part, up_far))
    part = product(place, normed, up_weight, up_probe, up_far, 1)
    forward, _ = reduce_z(part)
    backward_wide, backward_narrow, backward_taken = meet(backward, wide, narrow)
    forward_wide, forward_narrow, forward_taken = meet(forward, wide, narrow)

    blocks = gather_z(all_parts(forward_wide, backward_wide))
    forward_taken = after(forward_taken, blocks[1])
    mine = all_parts(forward_narrow + forward_taken.astype(F32), backward_narrow + backward_taken.astype(F32))
    both = jnp.concatenate([mine, send(mine, PARTNER)], axis=1)
    down_sent, down_own = wide_gradients(place, cot, blocks, 2 * wide, down_probe, down_far, 0)
    up_sent, up_own = wide_gradients(place, normed, blocks, 0, up_probe, up_far, 1)
    down_outs, up_outs = down_own(up_sent), up_own(up_sent)
    blocks = gather_z(after(both, blocks[3]))
    down_outs = place_taken(place, send(down_sent, PARTNER), down_outs, 0)
    outs = (*up_outs, *down_outs)
    return tuple(narrow_gradients(place, normed, cot, blocks, up_probe, down_probe, send(up_sent, PARTNER), outs))


def solution(mesh):
    in_specs = (
        P("tensor", "fsdp"),
        P("tensor", "fsdp"),
        P("fsdp", "tensor"),
        P("fsdp", "tensor"),
        P("tensor", "fsdp"),
        P("tensor", "fsdp"),
    )
    out_specs = (P("fsdp", "tensor"), P("fsdp", "tensor"), P("tensor", "fsdp"), P("tensor", "fsdp"))
    return jax.shard_map(
        on_device, mesh=mesh, in_specs=in_specs, out_specs=out_specs, check_vma=False
    )
```

```python
import jax
import jax.numpy as jnp
from jax import lax
from jax.experimental import pallas as pl
from jax.experimental.pallas import tpu as pltpu
from jax.sharding import PartitionSpec as P

epsilon = 1e-05
inv_root_two = 0.7071067811865476
inv_root_tau = 0.3989422804014327

BOTH = ("fsdp", "tensor")
F32 = jnp.float32
BF16 = jnp.bfloat16


def pairs_of(move):
    pairs = []
    for fsdp in range(16):
        for tensor in range(16):
            x, y, z, core = (tensor // 8) * 2 + fsdp % 2, (tensor // 2) % 4, fsdp // 2, tensor % 2
            x, y, z, core = move(x, y, z, core)
            target = (z % 8 * 2 + x % 2) * 16 + (x // 2) * 8 + y * 2 + core
            pairs.append((fsdp * 16 + tensor, target))
    return pairs


MAIN = pairs_of(lambda x, y, z, c: (x, y, z + 1 - 2 * c, c))
MINOR = pairs_of(lambda x, y, z, c: (x, y, z - 1 + 2 * c, c))
PARTNER = pairs_of(lambda x, y, z, c: (x ^ 1, y, z, c))
CORES = pairs_of(lambda x, y, z, c: (x, y, z, c ^ 1))
FIRST = [pairs_of(lambda x, y, z, c, k=k: (x ^ k, y, z, c)) for k in (1, 2, 3)]
SECOND = [pairs_of(lambda x, y, z, c, k=k: (x, y ^ k, z, c)) for k in (1, 2, 3)]
DOUBLING = [pairs_of(lambda x, y, z, c, k=k: (x, y, z ^ k, c)) for k in (1, 2)]
DOUBLING.append(pairs_of(lambda x, y, z, c: (x, y, z + (2 if z % 4 > 1 else -2) + 8, c)))


def send(value, pairs):
    return lax.ppermute(value, BOTH, pairs)


def add(one, two):
    return (one.astype(F32) + two.astype(F32)).astype(BF16)


ORDER = (0, -1, 1, -2, 2, -3, 3, -4)
HBM = pl.BlockSpec(memory_space=pltpu.HBM)
VMEM = pl.BlockSpec(memory_space=pltpu.VMEM)
SMEM = pl.BlockSpec(memory_space=pltpu.SMEM)


def call(kernel, outs, out_specs, scratch, args, specs, aliases=None, flops=0):
    return pl.pallas_call(
        kernel,
        out_shape=outs,
        in_specs=specs,
        out_specs=out_specs,
        scratch_shapes=scratch,
        input_output_aliases=aliases or {},
        compiler_params=pltpu.CompilerParams(vmem_limit_bytes=40 * 2**20),
        cost_estimate=pl.CostEstimate(flops=flops, bytes_accessed=1024, transcendentals=0),
    )(*args)


def shape(*dims, dtype=BF16):
    return jax.ShapeDtypeStruct(dims, dtype)


def run_copies(pairs, sems):
    copies = [pltpu.make_async_copy(src, dst, sems.at[i]) for i, (src, dst) in enumerate(pairs)]
    for copy in copies:
        copy.start()
    return copies


def wait_all(copies):
    for copy in copies:
        copy.wait()


def after(value, event):
    return lax.optimization_barrier((value, event))[0]


def widths(share):
    return share * 2 // 3, share - share * 2 // 3


def pack(place, weight, probe, axis):
    share = weight.shape[axis] // 2
    wide, _ = widths(share)
    dims = (wide, weight.shape[1]) if axis == 0 else (weight.shape[0], wide)

    def kernel(place_ref, weight_ref, probe_ref, out_ref, sems):
        units = pl.ds(pl.multiple_of((1 - place_ref[1]) * share, 128), wide)
        pairs = [
            (ref.at[units, :] if axis == 0 else ref.at[:, units], out_ref.at[k])
            for k, ref in enumerate((weight_ref, probe_ref))
        ]
        wait_all(run_copies(pairs, sems))

    scratch = [pltpu.SemaphoreType.DMA((2,))]
    return call(kernel, shape(2, *dims), HBM, scratch, (place, weight, probe), [SMEM, HBM, HBM])


def position(block_of, z, core):
    delta = lax.rem((1 - 2 * core) * (block_of - z) + 16, 8)
    return jnp.where(delta == 0, 0, jnp.where(delta <= 3, 2 * delta, 15 - 2 * delta))


def assemble(place, plane, other):
    rows, width = plane.shape[1:]

    def kernel(plane_ref, other_ref, out_ref):
        for j in range(8):
            for far in range(2):
                chip = (j % 4) * 4 + 2 * (j // 4) + far
                cols = slice(far * width, (far + 1) * width)
                for src, first in ((plane_ref, 0), (other_ref, 8)):
                    out_ref[(first + j) * rows : (first + j + 1) * rows, cols] = src[chip]

    return call(kernel, shape(16 * rows, 2 * width), VMEM, [], (plane, other), [VMEM, VMEM])


def to_own_order(src_ref, dst_ref, place_ref):
    rows = src_ref.shape[0] // 8
    for b in range(8):
        spot = pl.multiple_of(position(b, place_ref[0], place_ref[2]) * rows, 16)
        dst_ref[pl.ds(spot, rows), :] = src_ref[b * rows : (b + 1) * rows, :]


def contract(one, two, one_dim, two_dim):
    return lax.dot_general(one, two, (((one_dim,), (two_dim,)), ((), ())), preferred_element_type=F32)


def product(place, rows_in, weight, probe, far, axis):
    tokens, features = rows_in.shape[0], rows_in.shape[1] // 2
    share = weight.shape[axis] // 2
    wide, narrow = widths(share)

    def kernel(place_ref, rows_ref, weight_ref, probe_ref, far_ref, out_ref, rows):
        half = place_ref[1]
        starts = ((half * share, wide), (half * share + wide, narrow), ((1 - half) * share + wide, narrow))
        to_own_order(rows_ref, rows, place_ref)
        for k, ref in enumerate((weight_ref, probe_ref)):
            units = [pl.ds(pl.multiple_of(start, 128), count) for start, count in starts]
            parts = [ref[u, :] if axis == 0 else ref[:, u] for u in units]
            one, two, three = (contract(rows[:, :features], part, 1, 1 - axis) for part in parts)
            one += contract(rows[:, features:], far_ref[k], 1, 1 - axis)
            out_ref[:, k * wide : (k + 1) * wide] = one.astype(BF16)
            start = 2 * wide + k * narrow
            out_ref[:, start : start + narrow] = two.astype(BF16)
            out_ref[:, start + 2 * narrow : start + 3 * narrow] = three.astype(BF16)

    args = (place, rows_in, weight, probe, far)
    outs = [shape(tokens, 2 * wide + 4 * narrow), shape(*rows_in.shape)]
    return call(kernel, outs, [VMEM] * 2, [], args, [SMEM] + [VMEM] * 4)


def stack_blocks(refs, start, dst_ref):
    rows, width = dst_ref.shape[0] // 8, dst_ref.shape[1]
    for p, ref in enumerate(refs):
        dst_ref[p * rows : (p + 1) * rows, :] = ref[:, start : start + width]


def put(pairs, sems):
    wait_all(run_copies(pairs, sems))


def wide_gradients(place, rows_in, blocks, start, probe, far, axis):
    features = rows_in.shape[1] // 2
    share = probe.shape[axis] // 2
    wide, _ = widths(share)
    count = len(blocks)
    dims = (wide, features) if axis == 0 else (features, wide)

    def fill(dst, acts, block_rows, block_probe):
        if axis == 0:
            total = contract(acts[...], block_rows, 0, 0)
            grad, hess = total[:wide], total[wide:]
        else:
            total = contract(block_rows, acts[...], 0, 0)
            grad, hess = total[:, :wide], total[:, wide:]
        dst[0] = grad.astype(BF16)
        dst[1] = (block_probe.astype(F32) * hess).astype(BF16)

    def far_kernel(rows, far_ref, *rest):
        refs, (sent_ref, acts) = rest[:count], rest[count:]
        stack_blocks(refs, start, acts)
        fill(sent_ref, acts, rows[:, features:], far_ref[1])

    def own_kernel(place_ref, rows, probe_ref, acts, grad_out, hess_out, own, kept, sems):
        units = pl.ds(pl.multiple_of(place_ref[1] * share, 128), wide)
        at = lambda ref: ref.at[units, :] if axis == 0 else ref.at[:, units]
        wait_all(run_copies([(at(probe_ref), own)], sems))
        fill(kept, acts, rows[:, :features], own[...])
        put([(kept.at[k], at(ref)) for k, ref in enumerate((grad_out, hess_out))], sems)

    acts_shape = shape(rows_in.shape[0], 2 * wide)
    specs = [VMEM] * (2 + count)
    sent, acts = call(far_kernel, [shape(2, *dims), acts_shape], [VMEM] * 2, [], (rows_in, far, *blocks), specs)

    def own(event):
        whole = shape(*probe.shape)
        scratch = [pltpu.VMEM(dims, BF16), pltpu.VMEM((2, *dims), BF16), pltpu.SemaphoreType.DMA((2,))]
        args = (place, rows_in, probe, after(acts, event))
        return call(own_kernel, [whole, whole], [HBM, HBM], scratch, args, [SMEM, VMEM, HBM, VMEM])

    return sent, own


def narrow_gradients(place, normed, cot, blocks, up_probe, down_probe, taken, outs):
    tokens, features = normed.shape[0], normed.shape[1] // 2
    share = down_probe.shape[0] // 2
    wide, narrow = widths(share)
    count = len(blocks)

    def kernel(place_ref, up_rows, down_rows, up_ref, down_ref, taken_ref, *rest):
        refs, (*out_refs, acts, up_own, down_own, up_kept, down_kept, sems) = rest[:count], rest[count + 4 :]
        half = place_ref[1]
        places = [pl.ds(pl.multiple_of(h * share + wide, 128), narrow) for h in (half, 1 - half)]
        probes = [(up_ref.at[:, units], up_own.at[i]) for i, units in enumerate(places)]
        probes += [(down_ref.at[units, :], down_own.at[i]) for i, units in enumerate(places)]
        copies = run_copies(probes, sems)
        units = pl.ds(pl.multiple_of((1 - half) * share, 128), wide)
        puts = [pltpu.make_async_copy(taken_ref.at[k], out_refs[k].at[:, units], sems.at[8 + k]) for k in range(2)]
        for copy in puts:
            copy.start()
        stack_blocks(refs, 0, acts)
        wait_all(copies)
        copies = []
        for i, units in enumerate(places):
            start = i * 4 * narrow
            total = contract(up_rows[:, :features], acts[:, start : start + 2 * narrow], 0, 0)
            up_kept[2 * i] = total[:, :narrow].astype(BF16)
            up_kept[2 * i + 1] = (up_own[i].astype(F32) * total[:, narrow:]).astype(BF16)
            for k in range(2):
                copies.append(pltpu.make_async_copy(up_kept.at[2 * i + k], out_refs[k].at[:, units], sems.at[4 * i + k]))
                copies[-1].start()
            total = contract(acts[:, start + 2 * narrow : start + 4 * narrow], down_rows[:, :features], 0, 0)
            down_kept[2 * i] = total[:narrow].astype(BF16)
            down_kept[2 * i + 1] = (down_own[i].astype(F32) * total[narrow:]).astype(BF16)
            for k in range(2):
                copies.append(pltpu.make_async_copy(down_kept.at[2 * i + k], out_refs[2 + k].at[units, :], sems.at[4 * i + 2 + k]))
                copies[-1].start()
        wait_all(copies + puts)

    scratch = [
        pltpu.VMEM((tokens, 8 * narrow), BF16),
        pltpu.VMEM((2, features, narrow), BF16),
        pltpu.VMEM((2, narrow, features), BF16),
        pltpu.VMEM((4, features, narrow), BF16),
        pltpu.VMEM((4, narrow, features), BF16),
        pltpu.SemaphoreType.DMA((10,)),
    ]
    args = (place, normed, cot, up_probe, down_probe, taken, *blocks, *outs)
    specs = [SMEM, VMEM, VMEM, HBM, HBM, HBM] + [VMEM] * count + [HBM] * 4
    aliases = {6 + count + k: k for k in range(4)}
    return call(kernel, [shape(*o.shape) for o in outs], [HBM] * 4, scratch, args, specs, aliases)


def place_taken(place, taken, outs, axis):
    share = outs[0].shape[axis] // 2
    wide, _ = widths(share)

    def kernel(place_ref, taken_ref, *rest):
        refs, sems = rest[2:4], rest[4]
        units = pl.ds(pl.multiple_of((1 - place_ref[1]) * share, 128), wide)
        put([(taken_ref.at[k], ref.at[units, :] if axis == 0 else ref.at[:, units]) for k, ref in enumerate(refs)], sems)

    args = (place, taken, *outs)
    scratch = [pltpu.SemaphoreType.DMA((2,))]
    return call(kernel, [shape(*o.shape) for o in outs], [HBM] * 2, scratch, args, [SMEM] + [HBM] * 3, {2: 0, 3: 1})


def part_at(rows, step):
    count = rows.shape[0] // 8
    return lax.slice_in_dim(rows, ORDER.index(step) * count, (ORDER.index(step) + 1) * count, axis=0)


def reduce_z(part, gates=()):
    main, minor = part_at(part, -4), part_at(part, -3)
    marks = []
    for step in range(4):
        if step < len(gates) and gates[step] is not None:
            main, minor = after((main, minor), gates[step])
        main = send(main, MAIN)
        if step < 3:
            minor = send(minor, MINOR)
        marks.append((main, minor))
        if step < 3:
            main = add(main, part_at(part, 3 - step))
        if step < 2:
            minor = add(minor, part_at(part, step - 2))
    return main.astype(F32) + minor.astype(F32) + part_at(part, 0).astype(F32), marks


def gather_z(part):
    out, main, minor = [part], part, part
    for step in range(4):
        main = send(main, MAIN)
        out.append(main)
        if step < 3:
            minor = send(minor, MINOR)
            out.append(minor)
    return out


def normalize(tok, full_width, events):
    values = tok.astype(F32)
    sums = jnp.stack([jnp.sum(values, axis=1), jnp.sum(values * values, axis=1)])
    for i, pairs in enumerate(DOUBLING):
        if events[i] is not None:
            sums = after(sums, events[i])
        sums = sums + send(sums, pairs)
    mean = (sums[0] / full_width)[:, None]
    scale = lax.rsqrt((sums[1] / full_width)[:, None] - mean * mean + epsilon)
    return ((values - mean) * scale).astype(BF16)


def slopes(forward):
    width = forward.shape[1] // 2
    pre_act, tangent = forward[:, :width], forward[:, width:]
    cumulative = 0.5 * (1.0 + lax.erf(pre_act * inv_root_two))
    density = jnp.exp(-0.5 * pre_act * pre_act) * inv_root_tau
    slope = cumulative + pre_act * density
    curve = density * (2.0 - pre_act * pre_act)
    return pre_act, tangent, cumulative, slope, curve


def hidden_parts(forward):
    pre_act, tangent, cumulative, slope, _ = slopes(forward)
    return jnp.concatenate([(pre_act * cumulative).astype(BF16), (slope * tangent).astype(BF16)], axis=1)


def gradient_parts(forward, backward):
    _, tangent, _, slope, curve = slopes(forward)
    back_grad, tangent_back = jnp.split(backward, 2, axis=1)
    grad_pre = (back_grad * slope).astype(BF16)
    tangent_pre = (tangent_back * slope + back_grad * curve * tangent).astype(BF16)
    return jnp.concatenate([grad_pre, tangent_pre], axis=1)


def meet(total, wide, narrow):
    own, theirs = total[:, 2 * wide : 2 * wide + 2 * narrow], total[:, 2 * wide + 2 * narrow :]
    return total[:, : 2 * wide], own, send(theirs.astype(BF16), PARTNER)


def all_parts(forward, backward):
    return jnp.concatenate([gradient_parts(forward, backward), hidden_parts(forward)], axis=1)


def on_device(tokens, cotangent, up_weight, up_probe, down_weight, down_probe):
    full_width = tokens.shape[1] * lax.axis_size("fsdp")
    fsdp = lax.axis_index("fsdp")
    core = lax.axis_index("tensor") % 2
    place = jnp.stack([fsdp // 2, fsdp % 2, core]).astype(jnp.int32)
    wide, narrow = widths(up_weight.shape[1] // 2)

    rows = jnp.stack([tokens, cotangent])
    packed = pack(place, down_weight, down_probe, 0)
    line = jnp.stack([rows] + [send(rows, pairs) for pairs in FIRST])
    line, packed = lax.optimization_barrier((line, packed))
    down_far = send(packed, PARTNER)
    packed = pack(place, up_weight, up_probe, 1)
    plane = jnp.stack([line] + [send(line, pairs) for pairs in SECOND])
    plane = plane.reshape(16, *rows.shape)
    tok, cot = plane[:, 0], plane[:, 1]
    tok, packed = lax.optimization_barrier((tok, packed))
    up_far = send(packed, PARTNER)
    other = jnp.concatenate([send(half, CORES) for half in jnp.split(tok, 2)])
    tok = assemble(place, tok, other)
    cot = after(cot, (other, down_far))
    cot = assemble(place, cot, send(cot, CORES))
    part, cot = product(place, cot, down_weight, down_probe, down_far, 0)
    normed = normalize(tok, full_width, (None, part, up_far))
    backward, _ = reduce_z(after(part, up_far))
    part, normed = product(place, normed, up_weight, up_probe, up_far, 1)
    forward, _ = reduce_z(part)
    backward_wide, backward_narrow, backward_taken = meet(backward, wide, narrow)
    forward_wide, forward_narrow, forward_taken = meet(forward, wide, narrow)

    blocks = gather_z(all_parts(forward_wide, backward_wide))
    forward_taken = after(forward_taken, blocks[1])
    mine = all_parts(forward_narrow + forward_taken.astype(F32), backward_narrow + backward_taken.astype(F32))
    both = jnp.concatenate([mine, send(mine, PARTNER)], axis=1)
    down_sent, down_own = wide_gradients(place, cot, blocks, 2 * wide, down_probe, down_far, 0)
    up_sent, up_own = wide_gradients(place, normed, blocks, 0, up_probe, up_far, 1)
    down_outs, up_outs = down_own(up_sent), up_own(up_sent)
    blocks = gather_z(after(both, blocks[3]))
    down_outs = place_taken(place, send(down_sent, PARTNER), down_outs, 0)
    outs = (*up_outs, *down_outs)
    return tuple(narrow_gradients(place, normed, cot, blocks, up_probe, down_probe, send(up_sent, PARTNER), outs))


def solution(mesh):
    in_specs = (
        P("tensor", "fsdp"),
        P("tensor", "fsdp"),
        P("fsdp", "tensor"),
        P("fsdp", "tensor"),
        P("tensor", "fsdp"),
        P("tensor", "fsdp"),
    )
    out_specs = (P("fsdp", "tensor"), P("fsdp", "tensor"), P("tensor", "fsdp"), P("tensor", "fsdp"))
    return jax.shard_map(
        on_device, mesh=mesh, in_specs=in_specs, out_specs=out_specs, check_vma=False
    )
```
